32 devices in a mesh: grp: 2 (over x), mem: 16 (over z, y, core).
Axes of the slice: x: 2, y: 2, z: 4, core: 2. Of those that a mesh axis runs over, the one named last changes fastest.
Arguments:
- state_ens: bfloat16 [512, 16384], P('mem', 'grp'), may hold values from -6 to 6
- obs_ens: bfloat16 [512, 32768], P('mem', 'grp'), may hold values from -6 to 6
- obs_value: float32 [32768], P(('grp', 'mem')), may hold values from -12 to 12
- obs_class: int32 [32768], P(('grp', 'mem')), may hold values from 0 to 15
- loc_table: bfloat16 [16], replicated, may hold values from 0.049804688 to 1
- nbr_weight: float32 [4], replicated, may hold values from 0.25 to 1
Outputs:
- analysis: bfloat16 [512, 16384], P('mem', 'grp')
The draws below stay inside these ranges and needn't reach their ends.
All inputs are finite; a program needn't handle non-finite values.
Results may differ from the reference program's by a relative error of at most 0.0065.
Values may be sent and summed in bfloat16 or wider, within the bound.
A program may use at most 64 MiB of HBM per device.

```python
import math
import jax
import jax.numpy as jnp
from jax import lax

MEMBERS = 512
CELLS = 512
LOCAL_OBS = 1024
SWEEPS = 5
ROW_PATCHES = 8
CLASSES = 16
ALL_CELLS = 16384
ALL_OBS = 32768
N_GRP = 2
N_MEM = 16


def with_ends(array, rng, least, largest):
    extent = array.shape
    index_at = [jax.random.randint(jax.random.fold_in(rng, axis), (), 0, extent[axis]) for axis in range(len(extent))]
    array = array.at[tuple(index_at)].set(least)
    longest = extent.index(max(extent))
    index_at[longest] = (index_at[longest] + 1) % extent[longest]
    return array.at[tuple(index_at)].set(largest)


def steps_of(rng, extent, cuts, least, top_value):
    def one(axis_at, blocks):
        steps = jax.random.uniform(jax.random.fold_in(jax.random.fold_in(rng, 6), axis_at), (blocks,), jnp.float32, least / len(cuts), top_value / len(cuts))
        return jnp.repeat(jnp.exp(steps), extent[axis_at] // blocks).reshape((-1,) + (1,) * (len(extent) - axis_at - 1))

    level = one(*cuts[0])
    for cut in cuts[1:]:
        level = level * one(*cut)
    return level


def centred(key, shape, scale, limit, split=(), held_as=jnp.bfloat16):
    drawn = scale * jax.random.normal(key, shape, jnp.float32)
    if split:
        drawn = drawn * steps_of(key, shape, split, -0.22, 0.18)
    return jnp.clip(drawn, -limit, limit).astype(held_as)


def setup_inputs(seed: int = 0) -> dict:
    arg_keys = jax.random.split(jax.random.key(seed), 7)
    return {
        "state_ens": centred(arg_keys[0], (MEMBERS, ALL_CELLS), 1.0, 6.0, ((0, 16), (1, 2))),
        "obs_ens": centred(arg_keys[1], (MEMBERS, ALL_OBS), 1.0, 6.0, ((0, 16), (1, 2))),
        "obs_value": centred(arg_keys[2], (ALL_OBS,), 2.0, 12.0, ((0, 32),), jnp.float32),
        "obs_class": with_ends(jax.random.randint(arg_keys[3], (ALL_OBS,), 0, CLASSES), jax.random.fold_in(arg_keys[3], 1), 0, CLASSES - 1).astype(jnp.int32),
        "loc_table": jnp.clip(jnp.exp(jax.random.uniform(arg_keys[4], (CLASSES,), jnp.float32, math.log(0.049804688), math.log(1.0))), 0.049804688, 1.0).astype(jnp.bfloat16),
        "nbr_weight": jnp.clip(jax.random.uniform(arg_keys[5], (4,), jnp.float32, 0.25, 1.0), 0.25, 1.0),
    }


def mirror(product):
    return jnp.triu(product) + jnp.triu(product, 1).T

def newton_root(system):
    norm_total = jnp.sqrt(jnp.sum(system * system))
    identity = jnp.eye(system.shape[0], dtype=jnp.float32)
    iterate = system / norm_total
    root_inv = identity
    for sweep in range(SWEEPS):
        middle = 1.5 * identity - 0.5 * jnp.dot(root_inv, iterate, precision=lax.Precision.HIGHEST)
        iterate = jnp.dot(iterate, middle, precision=lax.Precision.HIGHEST)
        root_inv = jnp.dot(middle, root_inv, precision=lax.Precision.HIGHEST)
    return (root_inv, norm_total)

def reference(state_ens, obs_ens, obs_value, obs_class, loc_table, nbr_weight):
    patches = N_GRP * N_MEM

    def own_terms(index):
        start = (index * LOCAL_OBS).astype(jnp.int32)
        obs_block = lax.dynamic_slice_in_dim(obs_ens, start, LOCAL_OBS, 1)
        observed = lax.dynamic_slice_in_dim(obs_value, start, LOCAL_OBS, 0)
        classes = lax.dynamic_slice_in_dim(obs_class, start, LOCAL_OBS, 0)
        centre = lax.optimization_barrier(jnp.sum(obs_block, axis=0, dtype=jnp.float32)) / MEMBERS
        spread = (obs_block.astype(jnp.float32) - centre).astype(jnp.bfloat16)
        rates = loc_table[classes]
        scaled = (spread.astype(jnp.float32) * rates.astype(jnp.float32)).astype(jnp.bfloat16)
        innovation = (rates.astype(jnp.float32) * (observed - centre)).astype(jnp.bfloat16)
        gram_own = mirror(jnp.dot(spread, scaled.T, preferred_element_type=jnp.float32))
        vector_own = jnp.dot(spread, innovation, preferred_element_type=jnp.float32)
        return (gram_own, vector_own)
    grams, vectors = lax.map(own_terms, jnp.arange(patches, dtype=jnp.int32))

    def analyse(index):
        column = index % ROW_PATCHES
        system = grams[index] + (MEMBERS - 1.0) * jnp.eye(MEMBERS, dtype=jnp.float32)
        rhs_vector = vectors[index]
        links = ((1, 0, column != 0), (-1, 1, column != ROW_PATCHES - 1), (ROW_PATCHES, 2, column >= 0), (-ROW_PATCHES, 3, column >= 0))
        for offset, direction, active in links:
            source = index - offset
            inside = jnp.logical_and(jnp.logical_and(source >= 0, source < patches), active)
            clipped = jnp.clip(source, 0, patches - 1).astype(jnp.int32)
            factor = nbr_weight[direction] * inside.astype(jnp.float32)
            system = system + factor * grams[clipped]
            rhs_vector = rhs_vector + factor * vectors[clipped]
        root_inv, norm_total = newton_root(system)
        half_step = jnp.dot(root_inv, rhs_vector, precision=lax.Precision.HIGHEST)
        mean_weight = jnp.dot(root_inv, half_step, precision=lax.Precision.HIGHEST) / norm_total
        transform = (jnp.sqrt((MEMBERS - 1.0) / norm_total) * root_inv + mean_weight[:, None]).astype(jnp.bfloat16)
        start = (index * CELLS).astype(jnp.int32)
        states = lax.dynamic_slice_in_dim(state_ens, start, CELLS, 1)
        centre = lax.optimization_barrier(jnp.sum(states, axis=0, dtype=jnp.float32)) / MEMBERS
        deviation = (states.astype(jnp.float32) - centre).astype(jnp.bfloat16)
        update = lax.dot_general(transform, deviation, (((0,), (0,)), ((), ())), preferred_element_type=jnp.float32)
        return (centre + update).astype(jnp.bfloat16)
    blocks = lax.map(analyse, jnp.arange(patches, dtype=jnp.int32))
    return jnp.transpose(blocks, (1, 0, 2)).reshape(MEMBERS, patches * CELLS)
```

```python
import functools
import jax
import jax.numpy as jnp
from jax import lax
from jax.experimental import pallas as pl
from jax.experimental.pallas import tpu as pltpu
from jax.sharding import PartitionSpec as P

SWEEPS = 5
ROW_PATCHES = 8
CORES = 2
BLOCK = 128
BF16 = jnp.bfloat16
F32 = jnp.float32
MESH = pl.DeviceIdType.MESH


class Grid:
    def __init__(self, groups, members):
        self.groups, self.members = groups, members
        self.rows = members // ROW_PATCHES
        self.slabs = ROW_PATCHES // CORES
        self.slab = members // self.slabs

    def split(self, mem):
        return mem // self.slab, (mem % self.slab) // CORES, mem % CORES

    def join(self, z, y, core):
        return z * self.slab + y * CORES + core

    def flip(self, group, row):
        return row + (group % 2) * (self.rows - 1 - 2 * row)

    def patch(self, group, mem):
        z, y, core = self.split(mem)
        return self.flip(group, y) * ROW_PATCHES + z * CORES + core

    def holder(self, group, patch):
        row, column = patch // ROW_PATCHES, patch % ROW_PATCHES
        return self.join(column // CORES, self.flip(group, row), column % CORES)

    def steps(self):
        order = [2, 1, 3, 0] if self.slabs == 4 else list(range(self.slabs))[::-1]
        return [
            (dz, [(dy, dc) for dy in range(self.rows) for dc in range(CORES) if (dz, dy, dc) != (0, 0, 0)])
            for dz in order
        ]

    def peer(self, mem, dz, dy, dc):
        z, y, core = self.split(mem)
        return self.join((z + dz) % self.slabs, (y + dy) % self.rows, (core + dc) % CORES)


def halves(value):
    high = value.astype(BF16)
    return high, (value - high.astype(F32)).astype(BF16)


def dot(a, b):
    return jnp.dot(a, b, preferred_element_type=F32)


def kernel(
    grid, weights, table, value_ref, class_ref, state_ref, obs_ref, out_ref,
    obs_in, state_in, value_in, class_in, spread, scaled, send, got, system,
    wh, wl, mh, ml, zh, zl, th, tl, ana,
    local_sems, meta_sems, obs_send, obs_recv, state_send, state_recv,
    gram_send, gram_recv, out_send, out_recv,
):
    group, mem = lax.axis_index("grp"), lax.axis_index("mem")
    members = system.shape[0]
    rows = obs_in.shape[1]
    wide, cells = obs_in.shape[2], state_in.shape[2]
    z, y, core = grid.split(mem)
    row, column = grid.flip(group, y), z * CORES + core
    all_row = group * grid.rows + row
    last_row = grid.groups * grid.rows - 1
    steps = grid.steps()
    flat = [(dz, dy, dc) for dz, inner in steps for dy, dc in inner]

    north_row, south_row = jnp.maximum(all_row - 1, 0), jnp.minimum(all_row + 1, last_row)
    north_group, south_group = north_row // grid.rows, south_row // grid.rows
    west, east = jnp.maximum(column - 1, 0), jnp.minimum(column + 1, ROW_PATCHES - 1)
    neighbours = (
        (column > 0, (group, grid.join(west // CORES, y, west % CORES))),
        (column < ROW_PATCHES - 1, (group, grid.join(east // CORES, y, east % CORES))),
        (all_row > 0, (north_group, grid.join(z, grid.flip(north_group, north_row % grid.rows), core))),
        (all_row < last_row, (south_group, grid.join(z, grid.flip(south_group, south_row % grid.rows), core))),
    )

    barrier = pltpu.get_barrier_semaphore()
    for step in flat:
        pl.semaphore_signal(barrier, inc=1, device_id=(group, grid.peer(mem, *step)), device_id_type=MESH)
    for there, far in ((north_group, neighbours[2][1]), (south_group, neighbours[3][1])):

        @pl.when(there != group)
        def _():
            pl.semaphore_signal(barrier, inc=1, device_id=far, device_id_type=MESH)

    outside = (all_row - north_row) * (group - north_group) + (south_row - all_row) * (south_group - group)
    pl.semaphore_wait(barrier, len(flat) + outside)

    def columns_of(device, width):
        return pl.ds(pl.multiple_of(grid.patch(group, device) * width, BLOCK), width)

    def obs_copy(k):
        to = grid.peer(mem, *flat[k])
        return pltpu.make_async_remote_copy(
            src_ref=obs_ref.at[:, columns_of(to, wide)], dst_ref=obs_in.at[mem],
            send_sem=obs_send.at[k], recv_sem=obs_recv.at[k], device_id=(group, to), device_id_type=MESH)

    def state_copy(k):
        to = grid.peer(mem, *flat[k])
        return pltpu.make_async_remote_copy(
            src_ref=state_ref.at[:, columns_of(to, cells)], dst_ref=state_in.at[mem],
            send_sem=state_send.at[k], recv_sem=state_recv.at[k], device_id=(group, to), device_id_type=MESH)

    def out_copy(k):
        to = grid.peer(mem, *flat[k])
        return pltpu.make_async_remote_copy(
            src_ref=ana.at[to], dst_ref=out_ref.at[:, columns_of(mem, cells)],
            send_sem=out_send.at[k], recv_sem=out_recv.at[k], device_id=(group, to), device_id_type=MESH)

    meta_to = grid.holder(group, mem)
    meta_pairs = ((value_ref, value_in), (class_ref, class_in))

    def meta_copy(k):
        return pltpu.make_async_remote_copy(
            src_ref=meta_pairs[k][0], dst_ref=meta_pairs[k][1], send_sem=meta_sems.at[0, k],
            recv_sem=meta_sems.at[1, k], device_id=(group, meta_to), device_id_type=MESH)

    def meta_local(k):
        return pltpu.make_async_copy(meta_pairs[k][0], meta_pairs[k][1], meta_sems.at[1, k])

    @pl.when(meta_to != mem)
    def _():
        for k in range(2):
            meta_copy(k).start()

    @pl.when(meta_to == mem)
    def _():
        for k in range(2):
            meta_local(k).start()

    own_obs = pltpu.make_async_copy(obs_ref.at[:, columns_of(mem, wide)], obs_in.at[mem], local_sems.at[0])
    own_state = pltpu.make_async_copy(state_ref.at[:, columns_of(mem, cells)], state_in.at[mem], local_sems.at[1])
    for k in range(len(flat)):
        obs_copy(k).start()
    own_obs.start()
    own_state.start()

    @pl.when(meta_to != mem)
    def _():
        for k in range(2):
            meta_copy(k).wait()

    @pl.when(meta_to == mem)
    def _():
        for k in range(2):
            meta_local(k).wait()

    rates = jnp.zeros(class_in.shape, F32)
    for code in range(table.shape[0]):
        rates = jnp.where(class_in[...] == code, table[code], rates)

    own_obs.wait()
    for k in range(len(flat)):
        obs_copy(k).wait_recv()

    def add_up(source, width):
        def body(i, total):
            return total + jnp.sum(source[i].astype(F32), axis=0, keepdims=True)

        return lax.fori_loop(0, grid.members, body, jnp.zeros((1, width), F32)) / members

    centre = add_up(obs_in, wide)

    def spread_body(i, carry):
        block = (obs_in[i].astype(F32) - centre).astype(BF16)
        spread[i] = block
        scaled[i] = (block.astype(F32) * rates).astype(BF16)
        return carry

    lax.fori_loop(0, grid.members, spread_body, 0)
    innovation = (rates * (value_in[...] - centre)).astype(BF16)

    blocks = members // BLOCK
    pairs = [(i, j) for i in range(blocks) for j in range(i, blocks)]
    all_spread = spread[...].reshape(members, wide)
    all_scaled = scaled[...].reshape(members, wide)
    vector = lax.dot_general(
        jnp.broadcast_to(innovation, (16, wide)), all_spread, (((1,), (1,)), ((), ())), preferred_element_type=F32)[:1]
    pieces = jnp.concatenate(
        [vector[:, b * BLOCK:(b + 1) * BLOCK] for b in range(blocks)]
        + [jnp.zeros((8 - blocks, BLOCK), F32)], axis=0)
    pieces_high = pieces.astype(BF16).astype(F32)
    tail = len(pairs) * BLOCK
    send[tail:tail + 16, :] = jnp.concatenate([pieces_high, pieces - pieces_high], axis=0).astype(BF16)
    part = 2 * BLOCK
    for start in range(0, members, part):
        stripe = lax.dot_general(
            all_spread[start:start + part], all_scaled[start:], (((1,), (1,)), ((), ())), preferred_element_type=F32)
        system[start:start + part, start:] = stripe
        for index, (i, j) in enumerate(pairs):
            if start <= i * BLOCK < start + part:
                at = i * BLOCK - start
                piece = stripe[at:at + BLOCK, j * BLOCK - start:(j + 1) * BLOCK - start]
                send[index * BLOCK:(index + 1) * BLOCK, :] = piece.astype(BF16)

    opposite = (1, 0, 3, 2)

    def gram_copy(d):
        return pltpu.make_async_remote_copy(
            src_ref=send, dst_ref=got.at[opposite[d]], send_sem=gram_send.at[d],
            recv_sem=gram_recv.at[opposite[d]], device_id=neighbours[d][1], device_id_type=MESH)

    def gram_arrival(d):
        return pltpu.make_async_remote_copy(
            src_ref=send, dst_ref=got.at[d], send_sem=gram_send.at[d],
            recv_sem=gram_recv.at[d], device_id=neighbours[d][1], device_id_type=MESH)

    for d in (2, 3, 0, 1):

        @pl.when(neighbours[d][0])
        def _():
            gram_copy(d).start()

    for k in range(len(flat)):
        state_copy(k).start()

    rhs_ref = value_in
    rhs_ref[:, :members] = vector
    for d in (0, 1, 2, 3):

        @pl.when(neighbours[d][0])
        def _():
            gram_arrival(d).wait_recv()
            factor = weights[d]
            for index, (i, j) in enumerate(pairs):
                at = (slice(i * BLOCK, (i + 1) * BLOCK), slice(j * BLOCK, (j + 1) * BLOCK))
                system[at] = system[at] + factor * got[d, index * BLOCK:(index + 1) * BLOCK, :].astype(F32)
            extra = got[d, tail:tail + 16, :].astype(F32)
            both = extra[:8] + extra[8:]
            for b in range(blocks):
                at = (slice(0, 1), slice(b * BLOCK, (b + 1) * BLOCK))
                rhs_ref[at] = rhs_ref[at] + factor * both[b:b + 1]

    r_at = lax.broadcasted_iota(jnp.int32, (BLOCK, BLOCK), 0)
    c_at = lax.broadcasted_iota(jnp.int32, (BLOCK, BLOCK), 1)
    squares = jnp.zeros((BLOCK, BLOCK), F32)
    for i, j in pairs:
        rows_at, cols_at = slice(i * BLOCK, (i + 1) * BLOCK), slice(j * BLOCK, (j + 1) * BLOCK)
        piece = system[rows_at, cols_at]
        if i == j:
            piece = jnp.where(r_at <= c_at, piece, piece.T) + jnp.where(r_at == c_at, members - 1.0, 0.0)
            system[rows_at, cols_at] = piece
            squares = squares + piece * piece
        else:
            system[cols_at, rows_at] = piece.T
            squares = squares + 2.0 * (piece * piece)
    total = jnp.sum(jnp.sum(squares, axis=0, keepdims=True), axis=1, keepdims=True)
    norm = jnp.sqrt(total)
    inv_norm = 1.0 / norm

    def middle_of(part_value, start):
        shape = part_value.shape
        r = lax.broadcasted_iota(jnp.int32, shape, 0)
        c = lax.broadcasted_iota(jnp.int32, shape, 1) + start
        return jnp.where(r == c, 1.5, 0.0) - 0.5 * part_value

    chunks = [slice(start, start + part) for start in range(0, members, part)]

    def put(high_ref, low_ref, at, value):
        high, low = halves(value)
        high_ref[:, at] = high
        low_ref[:, at] = low

    def product(xh, xl, at):
        right_high = mh[:, at]
        return dot(xh[...], right_high) + dot(xl[...], right_high) + dot(xh[...], ml[:, at])

    for at in chunks:
        value = system[:, at] * inv_norm
        put(wh, wl, at, value)
        middle = middle_of(value, at.start)
        put(mh, ml, at, middle)
        put(zh, zl, at, middle)

    def advance():
        for at in chunks:
            put(th, tl, at, product(wh, wl, at))
        for at in chunks:
            system[:, at] = product(th, tl, at)
        for at in chunks:
            value = system[:, at]
            put(wh, wl, at, value)
            put(mh, ml, at, middle_of(value, at.start))

    advance()

    def sweep_body(sweep, carry):
        for at in chunks:
            put(th, tl, at, product(zh, zl, at))
        zh[...] = th[...]
        zl[...] = tl[...]
        advance()
        return carry

    lax.fori_loop(1, SWEEPS - 1, sweep_body, 0)
    for at in chunks:
        value = product(zh, zl, at)
        system[:, at] = value
        put(th, tl, at, value)

    def times_root(vec):
        high, low = halves(jnp.broadcast_to(vec, (16, members)))
        return (dot(high, th[...]) + dot(low, th[...]) + dot(high, tl[...]))[:1]

    mean = times_root(times_root(rhs_ref[:, :members])) * inv_norm
    scale = jnp.sqrt((members - 1.0) * inv_norm)

    own_state.wait()
    for k in range(len(flat)):
        state_copy(k).wait_recv()
    state_centre = add_up(state_in, cells)

    def deviation_body(i, carry):
        state_in[i] = (state_in[i].astype(F32) - state_centre).astype(BF16)
        return carry

    lax.fori_loop(0, grid.members, deviation_body, 0)
    deviation = state_in[...].reshape(members, cells)

    own_out = pltpu.make_async_copy(ana.at[mem], out_ref.at[:, columns_of(mem, cells)], local_sems.at[2])
    height = grid.slab * rows
    k = 0
    for dz, inner in steps:
        slab = (z + dz) % grid.slabs
        top = pl.multiple_of(slab * height, height)
        transform = (scale * system[pl.ds(top, height), :] + mean).astype(BF16)
        result = (state_centre + dot(transform, deviation)).astype(BF16)
        ana[pl.ds(slab * grid.slab, grid.slab)] = result.reshape(grid.slab, rows, cells)
        if dz == 0:
            own_out.start()
        for _ in inner:
            out_copy(k).start()
            k += 1

    own_out.wait()
    for k in range(len(flat)):
        out_copy(k).wait_recv()
    for k in range(len(flat)):
        obs_copy(k).wait_send()
        state_copy(k).wait_send()
        out_copy(k).wait_send()
    for d in range(4):

        @pl.when(neighbours[d][0])
        def _():
            gram_copy(d).wait_send()


def shards(grid, state_ens, obs_ens, obs_value, obs_class, loc_table, nbr_weight):
    rows = state_ens.shape[0]
    members = rows * grid.members
    wide, cells = obs_ens.shape[1] // grid.members, state_ens.shape[1] // grid.members
    blocks = members // BLOCK
    packed = blocks * (blocks + 1) // 2 * BLOCK + 16
    peers = grid.members - 1
    square = pltpu.VMEM((members, members), BF16)
    dma = pltpu.SemaphoreType.DMA
    vmem = pl.BlockSpec(memory_space=pltpu.VMEM)
    smem = pl.BlockSpec(memory_space=pltpu.SMEM)
    anywhere = pl.BlockSpec(memory_space=pl.ANY)
    return pl.pallas_call(
        functools.partial(kernel, grid),
        out_shape=jax.ShapeDtypeStruct(state_ens.shape, BF16),
        in_specs=[smem, smem, vmem, vmem, anywhere, anywhere],
        out_specs=anywhere,
        scratch_shapes=[
            pltpu.VMEM((grid.members, rows, wide), BF16),
            pltpu.VMEM((grid.members, rows, cells), BF16),
            pltpu.VMEM((1, wide), F32),
            pltpu.VMEM((1, wide), jnp.int32),
            pltpu.VMEM((grid.members, rows, wide), BF16),
            pltpu.VMEM((grid.members, rows, wide), BF16),
            pltpu.VMEM((packed, BLOCK), BF16),
            pltpu.VMEM((4, packed, BLOCK), BF16),
            pltpu.VMEM((members, members), F32),
        ]
        + [square] * 8
        + [
            pltpu.VMEM((grid.members, rows, cells), BF16),
            dma((3,)), dma((2, 2)), dma((peers,)), dma((peers,)), dma((peers,)), dma((peers,)),
            dma((4,)), dma((4,)), dma((peers,)), dma((peers,)),
        ],
        compiler_params=pltpu.CompilerParams(
            collective_id=0, has_side_effects=True, vmem_limit_bytes=48 * 1024 * 1024),
    )(nbr_weight, loc_table.astype(F32), obs_value[None, :], obs_class[None, :], state_ens, obs_ens)


def solution(mesh):
    grid = Grid(mesh.shape["grp"], mesh.shape["mem"])
    in_specs = (P("mem", "grp"), P("mem", "grp"), P(("grp", "mem")), P(("grp", "mem")), P(), P())
    return jax.shard_map(
        functools.partial(shards, grid), mesh=mesh, in_specs=in_specs, out_specs=P("mem", "grp"), check_vma=False)
```

```python
import functools
import jax
import jax.numpy as jnp
from jax import lax
from jax.experimental import pallas as pl
from jax.experimental.pallas import tpu as pltpu
from jax.sharding import PartitionSpec as P

SWEEPS = 5
ROW_PATCHES = 8
CORES = 2
BLOCK = 128
BF16 = jnp.bfloat16
F32 = jnp.float32
MESH = pl.DeviceIdType.MESH


class Grid:
    def __init__(self, groups, members):
        self.groups, self.members = groups, members
        self.rows = members // ROW_PATCHES
        self.slabs = ROW_PATCHES // CORES
        self.slab = members // self.slabs

    def split(self, mem):
        return mem // self.slab, (mem % self.slab) // CORES, mem % CORES

    def join(self, z, y, core):
        return z * self.slab + y * CORES + core

    def flip(self, group, row):
        return row + (group % 2) * (self.rows - 1 - 2 * row)

    def patch(self, group, mem):
        z, y, core = self.split(mem)
        return self.flip(group, y) * ROW_PATCHES + z * CORES + core

    def holder(self, group, patch):
        row, column = patch // ROW_PATCHES, patch % ROW_PATCHES
        return self.join(column // CORES, self.flip(group, row), column % CORES)

    def steps(self):
        order = [2, 1, 3, 0] if self.slabs == 4 else list(range(self.slabs))[::-1]
        return [
            (dz, [(dy, dc) for dy in range(self.rows) for dc in range(CORES) if (dz, dy, dc) != (0, 0, 0)])
            for dz in order
        ]

    def peer(self, mem, dz, dy, dc):
        z, y, core = self.split(mem)
        dz, dy, dc = dz % self.slabs, dy % self.rows, dc % CORES
        return self.join((z + dz) % self.slabs, (y + dy) % self.rows, (core + dc) % CORES)


def dot(a, b):
    return jnp.dot(a, b, preferred_element_type=F32)


def kernel(
    grid, classes, small_ref, value_ref, class_ref, state_ref, obs_ref, out_ref,
    small, obs_in, state_in, value_in, class_in, spread, scaled, send, got, system,
    wb, tb, zb_a, zb_b, mb_a, mb_b, wf, tf, zf, ana,
    local_sems, meta_sems, obs_send, obs_recv, state_send, state_recv,
    gram_send, gram_recv, out_send, out_recv,
):
    group, mem = lax.axis_index("grp"), lax.axis_index("mem")
    members = system.shape[0]
    rows = obs_in.shape[1]
    wide, cells = obs_in.shape[2], state_in.shape[2]
    z, y, core = grid.split(mem)
    row, column = grid.flip(group, y), z * CORES + core
    all_row = group * grid.rows + row
    last_row = grid.groups * grid.rows - 1
    steps = grid.steps()
    flat = [(dz, dy, dc) for dz, inner in steps for dy, dc in inner]

    north_row, south_row = jnp.maximum(all_row - 1, 0), jnp.minimum(all_row + 1, last_row)
    north_group, south_group = north_row // grid.rows, south_row // grid.rows
    west, east = jnp.maximum(column - 1, 0), jnp.minimum(column + 1, ROW_PATCHES - 1)
    neighbours = (
        (column > 0, (group, grid.join(west // CORES, y, west % CORES))),
        (column < ROW_PATCHES - 1, (group, grid.join(east // CORES, y, east % CORES))),
        (all_row > 0, (north_group, grid.join(z, grid.flip(north_group, north_row % grid.rows), core))),
        (all_row < last_row, (south_group, grid.join(z, grid.flip(south_group, south_row % grid.rows), core))),
    )

    barrier = pltpu.get_barrier_semaphore()
    for step in flat:
        pl.semaphore_signal(barrier, inc=1, device_id=(group, grid.peer(mem, *step)), device_id_type=MESH)
    for there, far in ((north_group, neighbours[2][1]), (south_group, neighbours[3][1])):

        @pl.when(there != group)
        def _():
            pl.semaphore_signal(barrier, inc=1, device_id=far, device_id_type=MESH)

    outside = (all_row - north_row) * (group - north_group) + (south_row - all_row) * (south_group - group)
    pl.semaphore_wait(barrier, len(flat) + outside)

    def columns_of(device, width):
        return pl.ds(pl.multiple_of(grid.patch(group, device) * width, BLOCK), width)

    def obs_copy(k):
        to = grid.peer(mem, *flat[k])
        return pltpu.make_async_remote_copy(
            src_ref=obs_ref.at[:, columns_of(to, wide)], dst_ref=obs_in.at[mem],
            send_sem=obs_send.at[k], recv_sem=obs_recv.at[k], device_id=(group, to), device_id_type=MESH)

    def state_copy(k):
        to = grid.peer(mem, *flat[k])
        return pltpu.make_async_remote_copy(
            src_ref=state_ref.at[:, columns_of(to, cells)], dst_ref=state_in.at[mem],
            send_sem=state_send.at[k], recv_sem=state_recv.at[k], device_id=(group, to), device_id_type=MESH)

    def out_copy(k):
        to = grid.peer(mem, *flat[k])
        return pltpu.make_async_remote_copy(
            src_ref=ana.at[to], dst_ref=out_ref.at[:, columns_of(mem, cells)],
            send_sem=out_send.at[k], recv_sem=out_recv.at[k], device_id=(group, to), device_id_type=MESH)

    meta_to = grid.holder(group, mem)
    meta_pairs = ((value_ref, value_in), (class_ref, class_in))

    def meta_copy(k):
        return pltpu.make_async_remote_copy(
            src_ref=meta_pairs[k][0], dst_ref=meta_pairs[k][1], send_sem=meta_sems.at[0, k],
            recv_sem=meta_sems.at[1, k], device_id=(group, meta_to), device_id_type=MESH)

    def meta_local(k):
        return pltpu.make_async_copy(meta_pairs[k][0], meta_pairs[k][1], meta_sems.at[1, k])

    @pl.when(meta_to != mem)
    def _():
        for k in range(2):
            meta_copy(k).start()

    @pl.when(meta_to == mem)
    def _():
        for k in range(2):
            meta_local(k).start()

    own_obs = pltpu.make_async_copy(obs_ref.at[:, columns_of(mem, wide)], obs_in.at[mem], local_sems.at[0])
    own_state = pltpu.make_async_copy(state_ref.at[:, columns_of(mem, cells)], state_in.at[mem], local_sems.at[1])
    for k in range(len(flat)):
        obs_copy(k).start()
    own_obs.start()
    own_small = pltpu.make_async_copy(small_ref, small, local_sems.at[3])
    own_small.start()
    own_small.wait()

    @pl.when(meta_to != mem)
    def _():
        for k in range(2):
            meta_copy(k).wait()

    @pl.when(meta_to == mem)
    def _():
        for k in range(2):
            meta_local(k).wait()

    rates = jnp.zeros(class_in.shape, F32)
    for code in range(classes):
        rates = jnp.where(class_in[...] == code, small[code], rates)

    def fold(block):
        value = block.astype(F32)
        if rows % 8:
            return jnp.sum(value, axis=0, keepdims=True)
        return jnp.sum(value.reshape(rows // 8, 8, value.shape[1]), axis=0)

    own_obs.wait()
    total = fold(obs_in[mem])
    for k in range(len(flat)):
        obs_copy(k).wait_recv()
        dz, dy, dc = flat[k]
        total = total + fold(obs_in[grid.peer(mem, -dz, -dy, -dc)])
    centre = jnp.sum(total, axis=0, keepdims=True) / members

    own_state.start()
    for k in range(len(flat)):
        state_copy(k).start()

    def spread_body(i, carry):
        block = (obs_in[i].astype(F32) - centre).astype(BF16)
        spread[i] = block
        scaled[i] = (block.astype(F32) * rates).astype(BF16)
        return carry

    lax.fori_loop(0, grid.members, spread_body, 0)
    innovation = (rates * (value_in[...] - centre)).astype(BF16)

    blocks = members // BLOCK
    pairs = [(i, j) for i in range(blocks) for j in range(i, blocks)]
    all_spread = spread[...].reshape(members, wide)
    all_scaled = scaled[...].reshape(members, wide)
    vector = lax.dot_general(
        jnp.broadcast_to(innovation, (16, wide)), all_spread, (((1,), (1,)), ((), ())), preferred_element_type=F32)[:1]
    pieces = jnp.concatenate(
        [vector[:, b * BLOCK:(b + 1) * BLOCK] for b in range(blocks)]
        + [jnp.zeros((8 - blocks, BLOCK), F32)], axis=0)
    pieces_high = pieces.astype(BF16).astype(F32)
    tail = len(pairs) * BLOCK
    send[tail:tail + 16, :] = jnp.concatenate([pieces_high, pieces - pieces_high], axis=0).astype(BF16)
    part = 2 * BLOCK
    for start in range(0, members, part):
        stripe = lax.dot_general(
            all_spread[start:start + part], all_scaled[start:], (((1,), (1,)), ((), ())), preferred_element_type=F32)
        system[start:start + part, start:] = stripe
        for index, (i, j) in enumerate(pairs):
            if start <= i * BLOCK < start + part:
                at = i * BLOCK - start
                piece = stripe[at:at + BLOCK, j * BLOCK - start:(j + 1) * BLOCK - start]
                send[index * BLOCK:(index + 1) * BLOCK, :] = piece.astype(BF16)

    opposite = (1, 0, 3, 2)

    def gram_copy(d):
        return pltpu.make_async_remote_copy(
            src_ref=send, dst_ref=got.at[opposite[d]], send_sem=gram_send.at[d],
            recv_sem=gram_recv.at[opposite[d]], device_id=neighbours[d][1], device_id_type=MESH)

    def gram_arrival(d):
        return pltpu.make_async_remote_copy(
            src_ref=send, dst_ref=got.at[d], send_sem=gram_send.at[d],
            recv_sem=gram_recv.at[d], device_id=neighbours[d][1], device_id_type=MESH)

    for d in (2, 3, 0, 1):

        @pl.when(neighbours[d][0])
        def _():
            gram_copy(d).start()

    rhs_ref = value_in
    rhs_ref[:, :members] = vector
    for d in (0, 1, 2, 3):

        @pl.when(neighbours[d][0])
        def _():
            gram_arrival(d).wait_recv()
            factor = small[classes + d]
            for index, (i, j) in enumerate(pairs):
                at = (slice(i * BLOCK, (i + 1) * BLOCK), slice(j * BLOCK, (j + 1) * BLOCK))
                system[at] = system[at] + factor * got[d, index * BLOCK:(index + 1) * BLOCK, :].astype(F32)
            extra = got[d, tail:tail + 16, :].astype(F32)
            both = extra[:8] + extra[8:]
            for b in range(blocks):
                at = (slice(0, 1), slice(b * BLOCK, (b + 1) * BLOCK))
                rhs_ref[at] = rhs_ref[at] + factor * both[b:b + 1]

    r_at = lax.broadcasted_iota(jnp.int32, (BLOCK, BLOCK), 0)
    c_at = lax.broadcasted_iota(jnp.int32, (BLOCK, BLOCK), 1)
    squares = jnp.zeros((BLOCK, BLOCK), F32)
    for i, j in pairs:
        rows_at, cols_at = slice(i * BLOCK, (i + 1) * BLOCK), slice(j * BLOCK, (j + 1) * BLOCK)
        piece = system[rows_at, cols_at]
        if i == j:
            piece = jnp.where(r_at <= c_at, piece, piece.T) + jnp.where(r_at == c_at, members - 1.0, 0.0)
            system[rows_at, cols_at] = piece
            squares = squares + piece * piece
        else:
            system[cols_at, rows_at] = piece.T
            squares = squares + 2.0 * (piece * piece)
    total = jnp.sum(jnp.sum(squares, axis=0, keepdims=True), axis=1, keepdims=True)
    norm = jnp.sqrt(total)
    inv_norm = 1.0 / norm

    def split_diagonal(value, start):
        pieces, diagonal = [], None
        for top in range(0, members, part):
            piece = value[top:top + part]
            if top == start:
                same = (
                    lax.broadcasted_iota(jnp.int32, piece.shape, 0)
                    == lax.broadcasted_iota(jnp.int32, piece.shape, 1))
                diagonal = jnp.sum(jnp.where(same, piece, 0.0), axis=0, keepdims=True)
                piece = jnp.where(same, 0.0, piece)
            pieces.append(piece)
        return diagonal, pieces

    chunks = [slice(start, start + part) for start in range(0, members, part)]

    def put_middle(middle_ref, value, at):
        diagonal, pieces = split_diagonal(value, at.start)
        for n, piece in enumerate(pieces):
            middle_ref[n * part:(n + 1) * part, at] = (-0.5 * piece).astype(BF16)
        return 1.5 - 0.5 * diagonal, pieces

    def product(x_full, x_half, middle_ref, diagonals, index):
        at = chunks[index]
        return x_full[:, at] * diagonals[index] + dot(x_half[...], middle_ref[:, at])

    diagonals = []
    for at in chunks:
        value = system[:, at] * inv_norm
        wf[:, at] = value
        wb[:, at] = value.astype(BF16)
        diagonal, pieces = put_middle(mb_a, value, at)
        diagonals.append(diagonal)
        for n, piece in enumerate(pieces):
            where = slice(n * part, (n + 1) * part)
            middle = -0.5 * piece
            if where == at:
                same = (
                    lax.broadcasted_iota(jnp.int32, piece.shape, 0)
                    == lax.broadcasted_iota(jnp.int32, piece.shape, 1))
                middle = jnp.where(same, diagonal, middle)
            zf[where, at] = middle
            zb_a[where, at] = middle.astype(BF16)

    def advance(middle, diagonals, later):
        for index, at in enumerate(chunks):
            value = product(wf, wb, middle, diagonals, index)
            tf[:, at] = value
            tb[:, at] = value.astype(BF16)
        result = []
        for index, at in enumerate(chunks):
            value = product(tf, tb, middle, diagonals, index)
            wf[:, at] = value
            wb[:, at] = value.astype(BF16)
            result.append(put_middle(later, value, at)[0])
        return result

    now, later = (zb_a, mb_a), (zb_b, mb_b)
    diagonals = advance(mb_a, diagonals, mb_b)
    now, later = (zb_a, mb_b), (zb_b, mb_a)
    for sweep in range(1, SWEEPS - 1):
        (z_now, m_now), (z_later, m_later) = now, later
        for index, at in enumerate(chunks):
            value = product(zf, z_now, m_now, diagonals, index)
            zf[:, at] = value
            z_later[:, at] = value.astype(BF16)
        diagonals = advance(m_now, diagonals, m_later)
        now, later = (z_later, m_later), (z_now, m_now)
    root_diagonals = []
    for index, at in enumerate(chunks):
        value = product(zf, now[0], now[1], diagonals, index)
        system[:, at] = value
        diagonal, pieces = split_diagonal(value, at.start)
        root_diagonals.append(diagonal)
        for n, piece in enumerate(pieces):
            tb[n * part:(n + 1) * part, at] = piece.astype(BF16)
    root_diagonal = jnp.concatenate(root_diagonals, axis=1)

    def times_root(vec):
        high = vec.astype(BF16).astype(F32)
        both = jnp.concatenate([high, vec - high, jnp.zeros((14, members), F32)], axis=0).astype(BF16)
        result = dot(both, tb[...])
        return vec * root_diagonal + result[0:1] + result[1:2]

    mean = times_root(times_root(rhs_ref[:, :members])) * inv_norm
    scale = jnp.sqrt((members - 1.0) * inv_norm)

    own_state.wait()
    total = fold(state_in[mem])
    for k in range(len(flat)):
        state_copy(k).wait_recv()
        dz, dy, dc = flat[k]
        total = total + fold(state_in[grid.peer(mem, -dz, -dy, -dc)])
    state_centre = jnp.sum(total, axis=0, keepdims=True) / members

    def deviation_body(i, carry):
        state_in[i] = (state_in[i].astype(F32) - state_centre).astype(BF16)
        return carry

    lax.fori_loop(0, grid.members, deviation_body, 0)
    deviation = state_in[...].reshape(members, cells)

    own_out = pltpu.make_async_copy(ana.at[mem], out_ref.at[:, columns_of(mem, cells)], local_sems.at[2])
    height = grid.slab * rows
    k = 0
    for dz, inner in steps:
        slab = (z + dz) % grid.slabs
        top = pl.multiple_of(slab * height, height)
        transform = (scale * system[pl.ds(top, height), :] + mean).astype(BF16)
        result = (state_centre + dot(transform, deviation)).astype(BF16)
        ana[pl.ds(slab * grid.slab, grid.slab)] = result.reshape(grid.slab, rows, cells)
        if dz == 0:
            own_out.start()
        for _ in inner:
            out_copy(k).start()
            k += 1

    own_out.wait()
    for k in range(len(flat)):
        out_copy(k).wait_recv()
    for k in range(len(flat)):
        obs_copy(k).wait_send()
        state_copy(k).wait_send()
        out_copy(k).wait_send()
    for d in range(4):

        @pl.when(neighbours[d][0])
        def _():
            gram_copy(d).wait_send()


def shards(grid, state_ens, obs_ens, obs_value, obs_class, loc_table, nbr_weight):
    rows = state_ens.shape[0]
    members = rows * grid.members
    wide, cells = obs_ens.shape[1] // grid.members, state_ens.shape[1] // grid.members
    blocks = members // BLOCK
    packed = blocks * (blocks + 1) // 2 * BLOCK + 16
    peers = grid.members - 1
    classes = loc_table.shape[0]
    small = jnp.concatenate([loc_table.astype(F32), nbr_weight, jnp.zeros((-(classes + 4) % BLOCK,), F32)])
    square = pltpu.VMEM((members, members), BF16)
    dma = pltpu.SemaphoreType.DMA
    anywhere = pl.BlockSpec(memory_space=pl.ANY)
    return pl.pallas_call(
        functools.partial(kernel, grid, classes),
        out_shape=jax.ShapeDtypeStruct(state_ens.shape, BF16),
        in_specs=[anywhere] * 5,
        out_specs=anywhere,
        scratch_shapes=[
            pltpu.SMEM(small.shape, F32),
            pltpu.VMEM((grid.members, rows, wide), BF16),
            pltpu.VMEM((grid.members, rows, cells), BF16),
            pltpu.VMEM((1, wide), F32),
            pltpu.VMEM((1, wide), jnp.int32),
            pltpu.VMEM((grid.members, rows, wide), BF16),
            pltpu.VMEM((grid.members, rows, wide), BF16),
            pltpu.VMEM((packed, BLOCK), BF16),
            pltpu.VMEM((4, packed, BLOCK), BF16),
            pltpu.VMEM((members, members), F32),
        ]
        + [square] * 6
        + [pltpu.VMEM((members, members), F32)] * 3
        + [
            pltpu.VMEM((grid.members, rows, cells), BF16),
            dma((4,)), dma((2, 2)), dma((peers,)), dma((peers,)), dma((peers,)), dma((peers,)),
            dma((4,)), dma((4,)), dma((peers,)), dma((peers,)),
        ],
        compiler_params=pltpu.CompilerParams(
            collective_id=0, has_side_effects=True, vmem_limit_bytes=62 * 1024 * 1024),
    )(small, obs_value[None, :], obs_class[None, :], state_ens, obs_ens)


def solution(mesh):
    grid = Grid(mesh.shape["grp"], mesh.shape["mem"])
    in_specs = (P("mem", "grp"), P("mem", "grp"), P(("grp", "mem")), P(("grp", "mem")), P(), P())
    return jax.shard_map(
        functools.partial(shards, grid), mesh=mesh, in_specs=in_specs, out_specs=P("mem", "grp"), check_vma=False)
```

```python
import functools
import jax
import jax.numpy as jnp
from jax import lax
from jax.experimental import pallas as pl
from jax.experimental.pallas import tpu as pltpu
from jax.sharding import PartitionSpec as P

SWEEPS = 5
ROW_PATCHES = 8
CORES = 2
BLOCK = 128
BF16 = jnp.bfloat16
F32 = jnp.float32
MESH = pl.DeviceIdType.MESH


class Grid:
    def __init__(self, groups, members):
        self.groups, self.members = groups, members
        self.rows = members // ROW_PATCHES
        self.slabs = ROW_PATCHES // CORES
        self.slab = members // self.slabs

    def split(self, mem):
        return mem // self.slab, (mem % self.slab) // CORES, mem % CORES

    def join(self, z, y, core):
        return z * self.slab + y * CORES + core

    def flip(self, group, row):
        return row + (group % 2) * (self.rows - 1 - 2 * row)

    def patch(self, group, mem):
        z, y, core = self.split(mem)
        return self.flip(group, y) * ROW_PATCHES + z * CORES + core

    def holder(self, group, patch):
        row, column = patch // ROW_PATCHES, patch % ROW_PATCHES
        return self.join(column // CORES, self.flip(group, row), column % CORES)

    def steps(self):
        order = [2, 1, 3, 0] if self.slabs == 4 else list(range(self.slabs))[::-1]
        return [
            (dz, [(dy, dc) for dy in range(self.rows) for dc in range(CORES) if (dz, dy, dc) != (0, 0, 0)])
            for dz in order
        ]

    def peer(self, mem, dz, dy, dc):
        z, y, core = self.split(mem)
        dz, dy, dc = dz % self.slabs, dy % self.rows, dc % CORES
        return self.join((z + dz) % self.slabs, (y + dy) % self.rows, (core + dc) % CORES)


def dot(a, b):
    return jnp.dot(a, b, preferred_element_type=F32)


def kernel(
    grid, weights, table, value_ref, class_ref, state_ref, obs_ref, out_ref,
    obs_in, state_in, value_in, class_in, spread, scaled, send, got, system,
    wb, tb, zb_a, zb_b, mb_a, mb_b, wf, tf, zf, ana,
    local_sems, meta_sems, obs_send, obs_recv, state_send, state_recv,
    gram_send, gram_recv, out_send, out_recv,
):
    group, mem = lax.axis_index("grp"), lax.axis_index("mem")
    members = system.shape[0]
    rows = obs_in.shape[1]
    wide, cells = obs_in.shape[2], state_in.shape[2]
    z, y, core = grid.split(mem)
    row, column = grid.flip(group, y), z * CORES + core
    all_row = group * grid.rows + row
    last_row = grid.groups * grid.rows - 1
    steps = grid.steps()
    flat = [(dz, dy, dc) for dz, inner in steps for dy, dc in inner]

    north_row, south_row = jnp.maximum(all_row - 1, 0), jnp.minimum(all_row + 1, last_row)
    north_group, south_group = north_row // grid.rows, south_row // grid.rows
    west, east = jnp.maximum(column - 1, 0), jnp.minimum(column + 1, ROW_PATCHES - 1)
    neighbours = (
        (column > 0, (group, grid.join(west // CORES, y, west % CORES))),
        (column < ROW_PATCHES - 1, (group, grid.join(east // CORES, y, east % CORES))),
        (all_row > 0, (north_group, grid.join(z, grid.flip(north_group, north_row % grid.rows), core))),
        (all_row < last_row, (south_group, grid.join(z, grid.flip(south_group, south_row % grid.rows), core))),
    )

    barrier = pltpu.get_barrier_semaphore()
    for step in flat:
        pl.semaphore_signal(barrier, inc=1, device_id=(group, grid.peer(mem, *step)), device_id_type=MESH)
    for there, far in ((north_group, neighbours[2][1]), (south_group, neighbours[3][1])):

        @pl.when(there != group)
        def _():
            pl.semaphore_signal(barrier, inc=1, device_id=far, device_id_type=MESH)

    outside = (all_row - north_row) * (group - north_group) + (south_row - all_row) * (south_group - group)
    pl.semaphore_wait(barrier, len(flat) + outside)

    def columns_of(device, width):
        return pl.ds(pl.multiple_of(grid.patch(group, device) * width, BLOCK), width)

    def obs_copy(k):
        to = grid.peer(mem, *flat[k])
        return pltpu.make_async_remote_copy(
            src_ref=obs_ref.at[:, columns_of(to, wide)], dst_ref=obs_in.at[mem],
            send_sem=obs_send.at[k], recv_sem=obs_recv.at[k], device_id=(group, to), device_id_type=MESH)

    def state_copy(k):
        to = grid.peer(mem, *flat[k])
        return pltpu.make_async_remote_copy(
            src_ref=state_ref.at[:, columns_of(to, cells)], dst_ref=state_in.at[mem],
            send_sem=state_send.at[k], recv_sem=state_recv.at[k], device_id=(group, to), device_id_type=MESH)

    def out_copy(k):
        to = grid.peer(mem, *flat[k])
        return pltpu.make_async_remote_copy(
            src_ref=ana.at[to], dst_ref=out_ref.at[:, columns_of(mem, cells)],
            send_sem=out_send.at[k], recv_sem=out_recv.at[k], device_id=(group, to), device_id_type=MESH)

    meta_to = grid.holder(group, mem)
    meta_pairs = ((value_ref, value_in), (class_ref, class_in))

    def meta_copy(k):
        return pltpu.make_async_remote_copy(
            src_ref=meta_pairs[k][0], dst_ref=meta_pairs[k][1], send_sem=meta_sems.at[0, k],
            recv_sem=meta_sems.at[1, k], device_id=(group, meta_to), device_id_type=MESH)

    def meta_local(k):
        return pltpu.make_async_copy(meta_pairs[k][0], meta_pairs[k][1], meta_sems.at[1, k])

    @pl.when(meta_to != mem)
    def _():
        for k in range(2):
            meta_copy(k).start()

    @pl.when(meta_to == mem)
    def _():
        for k in range(2):
            meta_local(k).start()

    own_obs = pltpu.make_async_copy(obs_ref.at[:, columns_of(mem, wide)], obs_in.at[mem], local_sems.at[0])
    own_state = pltpu.make_async_copy(state_ref.at[:, columns_of(mem, cells)], state_in.at[mem], local_sems.at[1])
    turns = sorted(range(len(flat)), key=lambda k: sum(flat[n][0] == flat[k][0] for n in range(k)))
    for k in turns:
        obs_copy(k).start()
    own_obs.start()

    @pl.when(meta_to != mem)
    def _():
        for k in range(2):
            meta_copy(k).wait()

    @pl.when(meta_to == mem)
    def _():
        for k in range(2):
            meta_local(k).wait()

    rates = jnp.zeros(class_in.shape, F32)
    for code in range(table.shape[0]):
        rates = jnp.where(class_in[...] == code, table[code], rates)

    def fold(block):
        value = block.astype(F32)
        if rows % 8:
            return jnp.sum(value, axis=0, keepdims=True)
        return jnp.sum(value.reshape(rows // 8, 8, value.shape[1]), axis=0)

    own_obs.wait()
    total = fold(obs_in[mem])
    for k in turns:
        obs_copy(k).wait_recv()
        dz, dy, dc = flat[k]
        total = total + fold(obs_in[grid.peer(mem, -dz, -dy, -dc)])
    centre = jnp.sum(total, axis=0, keepdims=True) / members

    own_state.start()
    for k in turns:
        if flat[k][1] == 0:
            state_copy(k).start()

    def spread_body(i, carry):
        block = (obs_in[i].astype(F32) - centre).astype(BF16)
        spread[i] = block
        scaled[i] = (block.astype(F32) * rates).astype(BF16)
        return carry

    lax.fori_loop(0, grid.members, spread_body, 0)
    innovation = (rates * (value_in[...] - centre)).astype(BF16)

    blocks = members // BLOCK
    pairs = [(i, j) for i in range(blocks) for j in range(i + 1)]
    all_spread = spread[...].reshape(members, wide)
    all_scaled = scaled[...].reshape(members, wide)
    left = jnp.concatenate([all_scaled, jnp.broadcast_to(innovation, (16, wide))], axis=0)
    part = 2 * BLOCK
    vectors = []
    for start in range(0, members, part):
        stripe = lax.dot_general(
            left[start:], all_spread[start:start + part], (((1,), (1,)), ((), ())), preferred_element_type=F32)
        vectors.append(stripe[members - start:members - start + 1])
        system[start:, start:start + part] = stripe[:members - start]
        for index, (i, j) in enumerate(pairs):
            if start <= j * BLOCK < start + part:
                at = j * BLOCK - start
                piece = stripe[i * BLOCK - start:(i + 1) * BLOCK - start, at:at + BLOCK]
                send[index * BLOCK:(index + 1) * BLOCK, :] = piece.astype(BF16)

    vector = jnp.concatenate(vectors, axis=1)
    pieces = jnp.concatenate(
        [vector[:, b * BLOCK:(b + 1) * BLOCK] for b in range(blocks)]
        + [jnp.zeros((8 - blocks, BLOCK), F32)], axis=0)
    pieces_high = pieces.astype(BF16).astype(F32)
    tail = len(pairs) * BLOCK
    send[tail:tail + 16, :] = jnp.concatenate([pieces_high, pieces - pieces_high], axis=0).astype(BF16)

    opposite = (1, 0, 3, 2)

    def gram_copy(d):
        return pltpu.make_async_remote_copy(
            src_ref=send, dst_ref=got.at[opposite[d]], send_sem=gram_send.at[d],
            recv_sem=gram_recv.at[opposite[d]], device_id=neighbours[d][1], device_id_type=MESH)

    def gram_arrival(d):
        return pltpu.make_async_remote_copy(
            src_ref=send, dst_ref=got.at[d], send_sem=gram_send.at[d],
            recv_sem=gram_recv.at[d], device_id=neighbours[d][1], device_id_type=MESH)

    for d in (2, 3, 0, 1):

        @pl.when(neighbours[d][0])
        def _():
            gram_copy(d).start()

    rhs_ref = value_in
    rhs_ref[:, :members] = vector
    for d in (0, 1, 2, 3):

        @pl.when(neighbours[d][0])
        def _():
            gram_arrival(d).wait_recv()
            factor = weights[d]
            for index, (i, j) in enumerate(pairs):
                at = (slice(i * BLOCK, (i + 1) * BLOCK), slice(j * BLOCK, (j + 1) * BLOCK))
                system[at] = system[at] + factor * got[d, index * BLOCK:(index + 1) * BLOCK, :].astype(F32)
            extra = got[d, tail:tail + 16, :].astype(F32)
            both = extra[:8] + extra[8:]
            for b in range(blocks):
                at = (slice(0, 1), slice(b * BLOCK, (b + 1) * BLOCK))
                rhs_ref[at] = rhs_ref[at] + factor * both[b:b + 1]

    for k in turns:
        if flat[k][1] != 0:
            state_copy(k).start()

    r_at = lax.broadcasted_iota(jnp.int32, (BLOCK, BLOCK), 0)
    c_at = lax.broadcasted_iota(jnp.int32, (BLOCK, BLOCK), 1)
    squares = jnp.zeros((BLOCK, BLOCK), F32)
    for i, j in pairs:
        rows_at, cols_at = slice(i * BLOCK, (i + 1) * BLOCK), slice(j * BLOCK, (j + 1) * BLOCK)
        piece = system[rows_at, cols_at]
        if i == j:
            piece = jnp.where(r_at >= c_at, piece, piece.T) + jnp.where(r_at == c_at, members - 1.0, 0.0)
            system[rows_at, cols_at] = piece
            squares = squares + piece * piece
        else:
            system[cols_at, rows_at] = piece.T
            squares = squares + 2.0 * (piece * piece)
    total = jnp.sum(jnp.sum(squares, axis=0, keepdims=True), axis=1, keepdims=True)
    norm = jnp.sqrt(total)
    inv_norm = 1.0 / norm

    def split_diagonal(value, start):
        pieces, diagonal = [], None
        for top in range(0, members, part):
            piece = value[top:top + part]
            if top == start:
                same = (
                    lax.broadcasted_iota(jnp.int32, piece.shape, 0)
                    == lax.broadcasted_iota(jnp.int32, piece.shape, 1))
                diagonal = jnp.sum(jnp.where(same, piece, 0.0), axis=0, keepdims=True)
                piece = jnp.where(same, 0.0, piece)
            pieces.append(piece)
        return diagonal, pieces

    chunks = [slice(start, start + part) for start in range(0, members, part)]

    def put_middle(middle_ref, value, at):
        diagonal, pieces = split_diagonal(value, at.start)
        for n, piece in enumerate(pieces):
            middle_ref[n * part:(n + 1) * part, at] = (-0.5 * piece).astype(BF16)
        return 1.5 - 0.5 * diagonal, pieces

    def product(x_full, x_half, middle_ref, diagonals, index):
        at = chunks[index]
        return x_full[:, at] * diagonals[index] + dot(x_half[...], middle_ref[:, at])

    diagonals = []
    for at in chunks:
        value = system[:, at] * inv_norm
        wf[:, at] = value
        wb[:, at] = value.astype(BF16)
        diagonal, pieces = put_middle(mb_a, value, at)
        diagonals.append(diagonal)
        for n, piece in enumerate(pieces):
            where = slice(n * part, (n + 1) * part)
            middle = -0.5 * piece
            if where == at:
                same = (
                    lax.broadcasted_iota(jnp.int32, piece.shape, 0)
                    == lax.broadcasted_iota(jnp.int32, piece.shape, 1))
                middle = jnp.where(same, diagonal, middle)
            zf[where, at] = middle
            zb_a[where, at] = middle.astype(BF16)

    def advance(middle, diagonals, later):
        for index, at in enumerate(chunks):
            value = product(wf, wb, middle, diagonals, index)
            tf[:, at] = value
            tb[:, at] = value.astype(BF16)
        result = []
        for index, at in enumerate(chunks):
            value = product(tf, tb, middle, diagonals, index)
            wf[:, at] = value
            wb[:, at] = value.astype(BF16)
            result.append(put_middle(later, value, at)[0])
        return result

    now, later = (zb_a, mb_a), (zb_b, mb_b)
    diagonals = advance(mb_a, diagonals, mb_b)
    now, later = (zb_a, mb_b), (zb_b, mb_a)
    for sweep in range(1, SWEEPS - 1):
        (z_now, m_now), (z_later, m_later) = now, later
        for index, at in enumerate(chunks):
            value = product(zf, z_now, m_now, diagonals, index)
            zf[:, at] = value
            z_later[:, at] = value.astype(BF16)
        diagonals = advance(m_now, diagonals, m_later)
        now, later = (z_later, m_later), (z_now, m_now)
    root_diagonals = []
    for index, at in enumerate(chunks):
        value = product(zf, now[0], now[1], diagonals, index)
        system[:, at] = value
        diagonal, pieces = split_diagonal(value, at.start)
        root_diagonals.append(diagonal)
        for n, piece in enumerate(pieces):
            tb[n * part:(n + 1) * part, at] = piece.astype(BF16)
    root_diagonal = jnp.concatenate(root_diagonals, axis=1)

    def times_root(vec):
        high = vec.astype(BF16).astype(F32)
        both = jnp.concatenate([high, vec - high, jnp.zeros((14, members), F32)], axis=0).astype(BF16)
        result = dot(both, tb[...])
        return vec * root_diagonal + result[0:1] + result[1:2]

    mean = times_root(times_root(rhs_ref[:, :members])) * inv_norm
    scale = jnp.sqrt((members - 1.0) * inv_norm)

    own_state.wait()
    total = fold(state_in[mem])
    for k in range(len(flat)):
        state_copy(k).wait_recv()
        dz, dy, dc = flat[k]
        total = total + fold(state_in[grid.peer(mem, -dz, -dy, -dc)])
    state_centre = jnp.sum(total, axis=0, keepdims=True) / members

    def deviation_body(i, carry):
        state_in[i] = (state_in[i].astype(F32) - state_centre).astype(BF16)
        return carry

    lax.fori_loop(0, grid.members, deviation_body, 0)
    deviation = state_in[...].reshape(members, cells)

    own_out = pltpu.make_async_copy(ana.at[mem], out_ref.at[:, columns_of(mem, cells)], local_sems.at[2])
    height = grid.slab * rows
    k = 0
    for dz, inner in steps:
        slab = (z + dz) % grid.slabs
        top = pl.multiple_of(slab * height, height)
        transform = (scale * system[pl.ds(top, height), :] + mean).astype(BF16)
        result = (state_centre + dot(transform, deviation)).astype(BF16)
        ana[pl.ds(slab * grid.slab, grid.slab)] = result.reshape(grid.slab, rows, cells)
        if dz == 0:
            own_out.start()
        for _ in inner:
            out_copy(k).start()
            k += 1

    own_out.wait()
    for k in range(len(flat)):
        out_copy(k).wait_recv()
    for k in range(len(flat)):
        obs_copy(k).wait_send()
        state_copy(k).wait_send()
        out_copy(k).wait_send()
    for d in range(4):

        @pl.when(neighbours[d][0])
        def _():
            gram_copy(d).wait_send()


def shards(grid, state_ens, obs_ens, obs_value, obs_class, loc_table, nbr_weight):
    rows = state_ens.shape[0]
    members = rows * grid.members
    wide, cells = obs_ens.shape[1] // grid.members, state_ens.shape[1] // grid.members
    blocks = members // BLOCK
    packed = blocks * (blocks + 1) // 2 * BLOCK + 16
    peers = grid.members - 1
    square = pltpu.VMEM((members, members), BF16)
    dma = pltpu.SemaphoreType.DMA
    smem = pl.BlockSpec(memory_space=pltpu.SMEM)
    anywhere = pl.BlockSpec(memory_space=pl.ANY)
    return pl.pallas_call(
        functools.partial(kernel, grid),
        out_shape=jax.ShapeDtypeStruct(state_ens.shape, BF16),
        in_specs=[smem] * 2 + [anywhere] * 4,
        out_specs=anywhere,
        scratch_shapes=[
            pltpu.VMEM((grid.members, rows, wide), BF16),
            pltpu.VMEM((grid.members, rows, cells), BF16),
            pltpu.VMEM((1, wide), F32),
            pltpu.VMEM((1, wide), jnp.int32),
            pltpu.VMEM((grid.members, rows, wide), BF16),
            pltpu.VMEM((grid.members, rows, wide), BF16),
            pltpu.VMEM((packed, BLOCK), BF16),
            pltpu.VMEM((4, packed, BLOCK), BF16),
            pltpu.VMEM((members, members), F32),
        ]
        + [square] * 6
        + [pltpu.VMEM((members, members), F32)] * 3
        + [
            pltpu.VMEM((grid.members, rows, cells), BF16),
            dma((3,)), dma((2, 2)), dma((peers,)), dma((peers,)), dma((peers,)), dma((peers,)),
            dma((4,)), dma((4,)), dma((peers,)), dma((peers,)),
        ],
        compiler_params=pltpu.CompilerParams(
            collective_id=0, has_side_effects=True, vmem_limit_bytes=62 * 1024 * 1024),
    )(nbr_weight, loc_table.astype(F32), obs_value[None, :], obs_class[None, :], state_ens, obs_ens)


def solution(mesh):
    grid = Grid(mesh.shape["grp"], mesh.shape["mem"])
    in_specs = (P("mem", "grp"), P("mem", "grp"), P(("grp", "mem")), P(("grp", "mem")), P(), P())
    return jax.shard_map(
        functools.partial(shards, grid), mesh=mesh, in_specs=in_specs, out_specs=P("mem", "grp"), check_vma=False)
```

```python
import functools
import jax
import jax.numpy as jnp
from jax import lax
from jax.experimental import pallas as pl
from jax.experimental.pallas import tpu as pltpu
from jax.sharding import PartitionSpec as P

SWEEPS = 5
ROW_PATCHES = 8
CORES = 2
BLOCK = 128
PARTS = 2
BF16 = jnp.bfloat16
F32 = jnp.float32
MESH = pl.DeviceIdType.MESH


class Grid:
    def __init__(self, groups, members):
        self.groups, self.members = groups, members
        self.rows = members // ROW_PATCHES
        self.slabs = ROW_PATCHES // CORES
        self.slab = members // self.slabs

    def split(self, mem):
        return mem // self.slab, (mem % self.slab) // CORES, mem % CORES

    def join(self, z, y, core):
        return z * self.slab + y * CORES + core

    def flip(self, group, row):
        return row + (group % 2) * (self.rows - 1 - 2 * row)

    def patch(self, group, mem):
        z, y, core = self.split(mem)
        return self.flip(group, y) * ROW_PATCHES + z * CORES + core

    def holder(self, group, patch):
        row, column = patch // ROW_PATCHES, patch % ROW_PATCHES
        return self.join(column // CORES, self.flip(group, row), column % CORES)

    def steps(self):
        order = [2, 1, 3, 0] if self.slabs == 4 else list(range(self.slabs))[::-1]
        return [
            (dz, [(dy, dc) for dy in range(self.rows) for dc in range(CORES) if (dz, dy, dc) != (0, 0, 0)])
            for dz in order
        ]

    def peer(self, mem, dz, dy, dc):
        z, y, core = self.split(mem)
        dz, dy, dc = dz % self.slabs, dy % self.rows, dc % CORES
        return self.join((z + dz) % self.slabs, (y + dy) % self.rows, (core + dc) % CORES)


def dot(a, b):
    return jnp.dot(a, b, preferred_element_type=F32)


def kernel(
    grid, weights, table, value_ref, class_ref, state_ref, obs_ref, out_ref,
    obs_in, state_in, value_in, class_in, spread, scaled, send, got, system,
    wb, tb, zb_a, zb_b, mb_a, mb_b, wf, tf, zf, ana,
    local_sems, meta_sems, obs_send, obs_recv, state_send, state_recv,
    gram_send, gram_recv, out_send, out_recv,
):
    group, mem = lax.axis_index("grp"), lax.axis_index("mem")
    members = system.shape[0]
    rows = obs_in.shape[2]
    half, cells = obs_in.shape[3], state_in.shape[2]
    wide = PARTS * half
    z, y, core = grid.split(mem)
    row, column = grid.flip(group, y), z * CORES + core
    all_row = group * grid.rows + row
    last_row = grid.groups * grid.rows - 1
    steps = grid.steps()
    flat = [(dz, dy, dc) for dz, inner in steps for dy, dc in inner]

    north_row, south_row = jnp.maximum(all_row - 1, 0), jnp.minimum(all_row + 1, last_row)
    north_group, south_group = north_row // grid.rows, south_row // grid.rows
    west, east = jnp.maximum(column - 1, 0), jnp.minimum(column + 1, ROW_PATCHES - 1)
    neighbours = (
        (column > 0, (group, grid.join(west // CORES, y, west % CORES))),
        (column < ROW_PATCHES - 1, (group, grid.join(east // CORES, y, east % CORES))),
        (all_row > 0, (north_group, grid.join(z, grid.flip(north_group, north_row % grid.rows), core))),
        (all_row < last_row, (south_group, grid.join(z, grid.flip(south_group, south_row % grid.rows), core))),
    )

    barrier = pltpu.get_barrier_semaphore()
    for step in flat:
        pl.semaphore_signal(barrier, inc=1, device_id=(group, grid.peer(mem, *step)), device_id_type=MESH)
    for there, far in ((north_group, neighbours[2][1]), (south_group, neighbours[3][1])):

        @pl.when(there != group)
        def _():
            pl.semaphore_signal(barrier, inc=1, device_id=far, device_id_type=MESH)

    outside = (all_row - north_row) * (group - north_group) + (south_row - all_row) * (south_group - group)
    pl.semaphore_wait(barrier, len(flat) + outside)

    def columns_of(device, width):
        return pl.ds(pl.multiple_of(grid.patch(group, device) * width, BLOCK), width)

    def obs_columns(device, h):
        return pl.ds(pl.multiple_of(grid.patch(group, device) * wide + h * half, BLOCK), half)

    def obs_copy(k, h):
        to = grid.peer(mem, *flat[k])
        return pltpu.make_async_remote_copy(
            src_ref=obs_ref.at[:, obs_columns(to, h)], dst_ref=obs_in.at[h, mem],
            send_sem=obs_send.at[h, k], recv_sem=obs_recv.at[h, k], device_id=(group, to), device_id_type=MESH)

    def own_obs(h):
        return pltpu.make_async_copy(obs_ref.at[:, obs_columns(mem, h)], obs_in.at[h, mem], local_sems.at[2 + h])

    def state_copy(k):
        to = grid.peer(mem, *flat[k])
        return pltpu.make_async_remote_copy(
            src_ref=state_ref.at[:, columns_of(to, cells)], dst_ref=state_in.at[mem],
            send_sem=state_send.at[k], recv_sem=state_recv.at[k], device_id=(group, to), device_id_type=MESH)

    def out_copy(k):
        to = grid.peer(mem, *flat[k])
        return pltpu.make_async_remote_copy(
            src_ref=ana.at[to], dst_ref=out_ref.at[:, columns_of(mem, cells)],
            send_sem=out_send.at[k], recv_sem=out_recv.at[k], device_id=(group, to), device_id_type=MESH)

    meta_to = grid.holder(group, mem)
    meta_pairs = ((value_ref, value_in), (class_ref, class_in))

    def meta_copy(k):
        return pltpu.make_async_remote_copy(
            src_ref=meta_pairs[k][0], dst_ref=meta_pairs[k][1], send_sem=meta_sems.at[0, k],
            recv_sem=meta_sems.at[1, k], device_id=(group, meta_to), device_id_type=MESH)

    def meta_local(k):
        return pltpu.make_async_copy(meta_pairs[k][0], meta_pairs[k][1], meta_sems.at[1, k])

    @pl.when(meta_to != mem)
    def _():
        for k in range(2):
            meta_copy(k).start()

    @pl.when(meta_to == mem)
    def _():
        for k in range(2):
            meta_local(k).start()

    own_state = pltpu.make_async_copy(state_ref.at[:, columns_of(mem, cells)], state_in.at[mem], local_sems.at[1])
    turns = sorted(range(len(flat)), key=lambda k: sum(flat[n][0] == flat[k][0] for n in range(k)))
    for h in range(PARTS):
        for k in turns:
            obs_copy(k, h).start()
        own_obs(h).start()

    @pl.when(meta_to != mem)
    def _():
        for k in range(2):
            meta_copy(k).wait()

    @pl.when(meta_to == mem)
    def _():
        for k in range(2):
            meta_local(k).wait()

    rates = jnp.zeros(class_in.shape, F32)
    for code in range(table.shape[0]):
        rates = jnp.where(class_in[...] == code, table[code], rates)

    def fold(block):
        value = block.astype(F32)
        if rows % 8:
            return jnp.sum(value, axis=0, keepdims=True)
        return jnp.sum(value.reshape(rows // 8, 8, value.shape[1]), axis=0)

    blocks = members // BLOCK
    pairs = [(i, j) for i in range(blocks) for j in range(i + 1)]
    part = 2 * BLOCK
    vectors = [0.0] * (members // part)
    for h in range(PARTS):
        at_h = slice(h * half, (h + 1) * half)
        own_obs(h).wait()
        total = fold(obs_in[h, mem])
        for k in turns:
            obs_copy(k, h).wait_recv()
            dz, dy, dc = flat[k]
            total = total + fold(obs_in[h, grid.peer(mem, -dz, -dy, -dc)])
        centre = jnp.sum(total, axis=0, keepdims=True) / members

        if h == PARTS - 1:
            own_state.start()
            for k in turns:
                if flat[k][1] == 0:
                    state_copy(k).start()

        def spread_body(i, carry):
            block = (obs_in[h, i].astype(F32) - centre).astype(BF16)
            spread[h, i] = block
            scaled[h, i] = (block.astype(F32) * rates[:, at_h]).astype(BF16)
            return carry

        lax.fori_loop(0, grid.members, spread_body, 0)
        innovation = (rates[:, at_h] * (value_in[:, at_h] - centre)).astype(BF16)
        all_spread = spread[h].reshape(members, half)
        all_scaled = scaled[h].reshape(members, half)
        left = jnp.concatenate([all_scaled, jnp.broadcast_to(innovation, (16, half))], axis=0)
        for n, start in enumerate(range(0, members, part)):
            stripe = lax.dot_general(
                left[start:], all_spread[start:start + part], (((1,), (1,)), ((), ())), preferred_element_type=F32)
            vectors[n] = vectors[n] + stripe[members - start:members - start + 1]
            stripe = stripe[:members - start]
            if h > 0:
                stripe = stripe + system[start:, start:start + part]
            system[start:, start:start + part] = stripe
            if h < PARTS - 1:
                continue
            for index, (i, j) in enumerate(pairs):
                if start <= j * BLOCK < start + part:
                    at = j * BLOCK - start
                    piece = stripe[i * BLOCK - start:(i + 1) * BLOCK - start, at:at + BLOCK]
                    send[index * BLOCK:(index + 1) * BLOCK, :] = piece.astype(BF16)

    vector = jnp.concatenate(vectors, axis=1)
    pieces = jnp.concatenate(
        [vector[:, b * BLOCK:(b + 1) * BLOCK] for b in range(blocks)]
        + [jnp.zeros((8 - blocks, BLOCK), F32)], axis=0)
    pieces_high = pieces.astype(BF16).astype(F32)
    tail = len(pairs) * BLOCK
    send[tail:tail + 16, :] = jnp.concatenate([pieces_high, pieces - pieces_high], axis=0).astype(BF16)

    opposite = (1, 0, 3, 2)

    def gram_copy(d):
        return pltpu.make_async_remote_copy(
            src_ref=send, dst_ref=got.at[opposite[d]], send_sem=gram_send.at[d],
            recv_sem=gram_recv.at[opposite[d]], device_id=neighbours[d][1], device_id_type=MESH)

    def gram_arrival(d):
        return pltpu.make_async_remote_copy(
            src_ref=send, dst_ref=got.at[d], send_sem=gram_send.at[d],
            recv_sem=gram_recv.at[d], device_id=neighbours[d][1], device_id_type=MESH)

    for d in (2, 3, 0, 1):

        @pl.when(neighbours[d][0])
        def _():
            gram_copy(d).start()

    rhs_ref = value_in
    rhs_ref[:, :members] = vector
    for d in (0, 1, 2, 3):

        @pl.when(neighbours[d][0])
        def _():
            gram_arrival(d).wait_recv()
            factor = weights[d]
            for index, (i, j) in enumerate(pairs):
                at = (slice(i * BLOCK, (i + 1) * BLOCK), slice(j * BLOCK, (j + 1) * BLOCK))
                system[at] = system[at] + factor * got[d, index * BLOCK:(index + 1) * BLOCK, :].astype(F32)
            extra = got[d, tail:tail + 16, :].astype(F32)
            both = extra[:8] + extra[8:]
            for b in range(blocks):
                at = (slice(0, 1), slice(b * BLOCK, (b + 1) * BLOCK))
                rhs_ref[at] = rhs_ref[at] + factor * both[b:b + 1]

    for k in turns:
        if flat[k][1] != 0:
            state_copy(k).start()

    r_at = lax.broadcasted_iota(jnp.int32, (BLOCK, BLOCK), 0)
    c_at = lax.broadcasted_iota(jnp.int32, (BLOCK, BLOCK), 1)
    squares = jnp.zeros((BLOCK, BLOCK), F32)
    for i, j in pairs:
        rows_at, cols_at = slice(i * BLOCK, (i + 1) * BLOCK), slice(j * BLOCK, (j + 1) * BLOCK)
        piece = system[rows_at, cols_at]
        if i == j:
            piece = jnp.where(r_at >= c_at, piece, piece.T) + jnp.where(r_at == c_at, members - 1.0, 0.0)
            system[rows_at, cols_at] = piece
            squares = squares + piece * piece
        else:
            system[cols_at, rows_at] = piece.T
            squares = squares + 2.0 * (piece * piece)
    total = jnp.sum(jnp.sum(squares, axis=0, keepdims=True), axis=1, keepdims=True)
    norm = jnp.sqrt(total)
    inv_norm = 1.0 / norm

    def split_diagonal(value, start):
        pieces, diagonal = [], None
        for top in range(0, members, part):
            piece = value[top:top + part]
            if top == start:
                same = (
                    lax.broadcasted_iota(jnp.int32, piece.shape, 0)
                    == lax.broadcasted_iota(jnp.int32, piece.shape, 1))
                diagonal = jnp.sum(jnp.where(same, piece, 0.0), axis=0, keepdims=True)
                piece = jnp.where(same, 0.0, piece)
            pieces.append(piece)
        return diagonal, pieces

    chunks = [slice(start, start + part) for start in range(0, members, part)]

    def put_middle(middle_ref, value, at):
        diagonal, pieces = split_diagonal(value, at.start)
        for n, piece in enumerate(pieces):
            middle_ref[n * part:(n + 1) * part, at] = (-0.5 * piece).astype(BF16)
        return 1.5 - 0.5 * diagonal, pieces

    def product(x_full, x_half, middle_ref, diagonals, index):
        at = chunks[index]
        return x_full[:, at] * diagonals[index] + dot(x_half[...], middle_ref[:, at])

    diagonals = []
    for at in chunks:
        value = system[:, at] * inv_norm
        wf[:, at] = value
        wb[:, at] = value.astype(BF16)
        diagonal, pieces = put_middle(mb_a, value, at)
        diagonals.append(diagonal)
        for n, piece in enumerate(pieces):
            where = slice(n * part, (n + 1) * part)
            middle = -0.5 * piece
            if where == at:
                same = (
                    lax.broadcasted_iota(jnp.int32, piece.shape, 0)
                    == lax.broadcasted_iota(jnp.int32, piece.shape, 1))
                middle = jnp.where(same, diagonal, middle)
            zf[where, at] = middle
            zb_a[where, at] = middle.astype(BF16)

    def advance(middle, diagonals, later):
        for index, at in enumerate(chunks):
            value = product(wf, wb, middle, diagonals, index)
            tf[:, at] = value
            tb[:, at] = value.astype(BF16)
        result = []
        for index, at in enumerate(chunks):
            value = product(tf, tb, middle, diagonals, index)
            wf[:, at] = value
            wb[:, at] = value.astype(BF16)
            result.append(put_middle(later, value, at)[0])
        return result

    now, later = (zb_a, mb_a), (zb_b, mb_b)
    diagonals = advance(mb_a, diagonals, mb_b)
    now, later = (zb_a, mb_b), (zb_b, mb_a)
    for sweep in range(1, SWEEPS - 1):
        (z_now, m_now), (z_later, m_later) = now, later
        for index, at in enumerate(chunks):
            value = product(zf, z_now, m_now, diagonals, index)
            zf[:, at] = value
            z_later[:, at] = value.astype(BF16)
        diagonals = advance(m_now, diagonals, m_later)
        now, later = (z_later, m_later), (z_now, m_now)
    root_diagonals = []
    for index, at in enumerate(chunks):
        value = product(zf, now[0], now[1], diagonals, index)
        system[:, at] = value
        diagonal, pieces = split_diagonal(value, at.start)
        root_diagonals.append(diagonal)
        for n, piece in enumerate(pieces):
            tb[n * part:(n + 1) * part, at] = piece.astype(BF16)
    root_diagonal = jnp.concatenate(root_diagonals, axis=1)

    def times_root(vec):
        high = vec.astype(BF16).astype(F32)
        both = jnp.concatenate([high, vec - high, jnp.zeros((14, members), F32)], axis=0).astype(BF16)
        result = dot(both, tb[...])
        return vec * root_diagonal + result[0:1] + result[1:2]

    mean = times_root(times_root(rhs_ref[:, :members])) * inv_norm
    scale = jnp.sqrt((members - 1.0) * inv_norm)

    own_state.wait()
    total = fold(state_in[mem])
    for k in range(len(flat)):
        state_copy(k).wait_recv()
        dz, dy, dc = flat[k]
        total = total + fold(state_in[grid.peer(mem, -dz, -dy, -dc)])
    state_centre = jnp.sum(total, axis=0, keepdims=True) / members

    def deviation_body(i, carry):
        state_in[i] = (state_in[i].astype(F32) - state_centre).astype(BF16)
        return carry

    lax.fori_loop(0, grid.members, deviation_body, 0)
    deviation = state_in[...].reshape(members, cells)

    own_out = pltpu.make_async_copy(ana.at[mem], out_ref.at[:, columns_of(mem, cells)], local_sems.at[0])
    height = grid.slab * rows
    k = 0
    for dz, inner in steps:
        slab = (z + dz) % grid.slabs
        top = pl.multiple_of(slab * height, height)
        transform = (scale * system[pl.ds(top, height), :] + mean).astype(BF16)
        result = (state_centre + dot(transform, deviation)).astype(BF16)
        ana[pl.ds(slab * grid.slab, grid.slab)] = result.reshape(grid.slab, rows, cells)
        if dz == 0:
            own_out.start()
        for _ in inner:
            out_copy(k).start()
            k += 1

    own_out.wait()
    for k in range(len(flat)):
        out_copy(k).wait_recv()
    for k in range(len(flat)):
        for h in range(PARTS):
            obs_copy(k, h).wait_send()
        state_copy(k).wait_send()
        out_copy(k).wait_send()
    for d in range(4):

        @pl.when(neighbours[d][0])
        def _():
            gram_copy(d).wait_send()


def shards(grid, state_ens, obs_ens, obs_value, obs_class, loc_table, nbr_weight):
    rows = state_ens.shape[0]
    members = rows * grid.members
    wide, cells = obs_ens.shape[1] // grid.members, state_ens.shape[1] // grid.members
    blocks = members // BLOCK
    packed = blocks * (blocks + 1) // 2 * BLOCK + 16
    peers = grid.members - 1
    square = pltpu.VMEM((members, members), BF16)
    dma = pltpu.SemaphoreType.DMA
    smem = pl.BlockSpec(memory_space=pltpu.SMEM)
    anywhere = pl.BlockSpec(memory_space=pl.ANY)
    return pl.pallas_call(
        functools.partial(kernel, grid),
        out_shape=pltpu.VMEM(state_ens.shape, BF16),
        in_specs=[smem] * 2 + [anywhere] * 4,
        out_specs=pl.BlockSpec(memory_space=pltpu.VMEM),
        scratch_shapes=[
            pltpu.VMEM((PARTS, grid.members, rows, wide // PARTS), BF16),
            pltpu.VMEM((grid.members, rows, cells), BF16),
            pltpu.VMEM((1, wide), F32),
            pltpu.VMEM((1, wide), jnp.int32),
            pltpu.VMEM((PARTS, grid.members, rows, wide // PARTS), BF16),
            pltpu.VMEM((PARTS, grid.members, rows, wide // PARTS), BF16),
            pltpu.VMEM((packed, BLOCK), BF16),
            pltpu.VMEM((4, packed, BLOCK), BF16),
            pltpu.VMEM((members, members), F32),
        ]
        + [square] * 6
        + [pltpu.VMEM((members, members), F32)] * 3
        + [
            pltpu.VMEM((grid.members, rows, cells), BF16),
            dma((2 + PARTS,)), dma((2, 2)), dma((PARTS, peers)), dma((PARTS, peers)), dma((peers,)), dma((peers,)),
            dma((4,)), dma((4,)), dma((peers,)), dma((peers,)),
        ],
        compiler_params=pltpu.CompilerParams(
            collective_id=0, has_side_effects=True, vmem_limit_bytes=60 * 1024 * 1024),
    )(nbr_weight, loc_table.astype(F32), obs_value[None, :], obs_class[None, :], state_ens, obs_ens)


def solution(mesh):
    grid = Grid(mesh.shape["grp"], mesh.shape["mem"])
    in_specs = (P("mem", "grp"), P("mem", "grp"), P(("grp", "mem")), P(("grp", "mem")), P(), P())
    return jax.shard_map(
        functools.partial(shards, grid), mesh=mesh, in_specs=in_specs, out_specs=P("mem", "grp"), check_vma=False)
```
